32 devices in a mesh: section: 4 (over y, x), half: 2 (over core), dp: 4 (over z).
Axes of the slice: x: 2, y: 2, z: 4, core: 2. Of those that a mesh axis runs over, the one named last changes fastest.
Arguments:
- query: bfloat16 [64, 12288], P('dp', ('section', 'half')), may hold values from -6 to 6
- train: bfloat16 [4096, 12288], P('dp', ('section', 'half')), may hold values from -0.0546875 to 0.0546875
- precond: bfloat16 [48, 256, 256], P(('section', 'half')), may hold values from -0.375 to 0.375
- module_kind: int32 [48], P(('section', 'half')), may hold values from 0 to 6
- kind_scale: float32 [7], replicated, may hold values from 0.25 to 4
Outputs:
- scores: float32 [64, 4096], P(('section', 'half'), 'dp')
The draws below stay inside these ranges and needn't reach their ends.
All inputs are finite; a program needn't handle non-finite values.
Results may differ from the reference program's by a relative error of at most 0.0029.
Values may be sent and summed in bfloat16 or wider, within the bound.
No kernel may reach another device: no remote copies, remote signals or barrier semaphores. Data moves between devices by JAX's collectives and lax.ppermute only.
A program may use at most 64 MiB of HBM per device.

```python
import math
import jax
import jax.numpy as jnp
from jax import lax

FEAT = 256
KINDS = 7
MODULES = 48
FEATURES = 12288
TRAIN = 4096
Q = 64


def with_ends(values, key, low, largest):
    extent = values.shape
    index_at = [jax.random.randint(jax.random.fold_in(key, axis), (), 0, extent[axis]) for axis in range(len(extent))]
    values = values.at[tuple(index_at)].set(low)
    longest = extent.index(max(extent))
    index_at[longest] = (index_at[longest] + 1) % extent[longest]
    return values.at[tuple(index_at)].set(largest)


def shard_levels(rng, shape, cuts, least, high):
    def one(dim, blocks):
        steps = jax.random.uniform(jax.random.fold_in(jax.random.fold_in(rng, 6), dim), (blocks,), jnp.float32, least / len(cuts), high / len(cuts))
        return jnp.repeat(jnp.exp(steps), shape[dim] // blocks).reshape((-1,) + (1,) * (len(shape) - dim - 1))

    gain = one(*cuts[0])
    for cut in cuts[1:]:
        gain = gain * one(*cut)
    return gain


def centred(own_key, dims, scale, most, shards=(), kind=jnp.bfloat16):
    result = jax.random.normal(own_key, dims, jnp.float32) * scale
    if len(shards) > 0:
        result = shard_levels(own_key, dims, shards, -0.22, 0.18) * result
    return jnp.clip(result, min=-most, max=most).astype(kind)


def setup_inputs(seed: int = 0) -> dict:
    key_list = jax.random.split(jax.random.key(seed), 6)
    query = centred(key_list[0], (Q, FEATURES), 1.0, 6.0, ((0, 4), (1, 8)))
    train = centred(key_list[1], (TRAIN, FEATURES), FEATURES ** -0.5, 0.0546875, ((0, 4), (1, 8)))
    precond = centred(key_list[2], (MODULES, FEAT, FEAT), FEAT ** -0.5, 0.375, ((0, 8),))
    module_kind = with_ends(jax.random.randint(key_list[3], (MODULES,), 0, KINDS), jax.random.fold_in(key_list[3], 1), 0, KINDS - 1).astype(jnp.int32)
    kind_scale = jnp.clip(jnp.exp(jax.random.uniform(key_list[4], (KINDS,), jnp.float32, math.log(0.25), math.log(4.0))), 0.25, 4.0)
    return {"query": query, "train": train, "precond": precond, "module_kind": module_kind, "kind_scale": kind_scale}


def reference(query, train, precond, module_kind, kind_scale):
    blocks = query.astype(jnp.float32).reshape(Q, MODULES, FEAT)
    pre = jnp.einsum("qmf,mfg->qmg", blocks, precond.astype(jnp.float32), precision=lax.Precision.HIGHEST)
    kinds = jnp.arange(KINDS, dtype=jnp.int32)
    onehot = (module_kind[:, None] == kinds[None, :]).astype(jnp.float32)
    factor = jnp.sum(onehot * kind_scale[None, :], axis=1)
    weighted = (pre * factor[None, :, None]).astype(jnp.bfloat16).reshape(Q, FEATURES)
    return lax.dot_general(weighted, train, (((1,), (1,)), ((), ())), preferred_element_type=jnp.float32)
```

```python
import functools

import jax
import jax.numpy as jnp
from jax import lax
from jax.experimental import pallas as pl
from jax.experimental.pallas import tpu as pltpu
from jax.sharding import PartitionSpec as P

SHARDS = ("section", "half")
DIRECT = 8
ROWS = 64


def local_scores(n, sections, halves, direct, *refs):
    blocks = refs[:n] if direct else refs[:1]
    train, precond, factor, keep, send = refs[len(blocks):]
    mods, feat = precond.shape[0], precond.shape[1]
    q_rows = blocks[0].shape[0] if direct else blocks[0].shape[0] // n
    out_rows = keep.shape[1]
    unit = min(q_rows, out_rows)
    dp, section, half = lax.axis_index("dp"), lax.axis_index("section"), lax.axis_index("half")

    def rows_of(first, rows, owners):
        parts = []
        for m in range(mods):
            cols = slice(m * feat, (m + 1) * feat)
            lhs = first(cols)
            pre = jnp.dot(lhs, precond[m], preferred_element_type=jnp.float32)
            parts.append((pre * factor[m]).astype(jnp.bfloat16))
        weighted = jnp.concatenate(parts, axis=1)
        scores = lax.dot_general(weighted, train[...], (((1,), (1,)), ((), ())), preferred_element_type=jnp.float32)
        for i in range(rows // unit):
            g = owners(i * unit)
            d, off = g // out_rows, pl.multiple_of(g % out_rows, unit)
            slot = lax.rem(d // halves, sections) ^ section
            value = scores[i * unit:(i + 1) * unit]
            mine = lax.rem(d, halves) == half

            @pl.when(mine)
            def _():
                keep[slot, pl.ds(off, unit), :] = value

            @pl.when(jnp.logical_not(mine))
            def _():
                send[slot, pl.ds(off, unit), :] = value

    if direct:
        first = lambda cols: jnp.concatenate([b[:, cols] for b in blocks], axis=0)
        rows_of(first, n * q_rows, lambda r: lax.rem(dp - r // q_rows + n, n) * q_rows + r % q_rows)
    else:
        def step(c, carry):
            base = pl.multiple_of(c * ROWS, ROWS)
            rows_of(lambda cols: blocks[0][pl.ds(base, ROWS), cols], ROWS, lambda r: base + r)
            return carry
        lax.fori_loop(0, n * q_rows // ROWS, step, 0)


def stage(train, precond, kind, scale, train_out, precond_out, factor_out, kind_s, scale_s, sems):
    pairs = ((kind, kind_s), (scale, scale_s), (precond, precond_out), (train, train_out))
    copies = [pltpu.make_async_copy(src, dst, sems.at[i]) for i, (src, dst) in enumerate(pairs)]
    for c in copies:
        c.start()
    copies[0].wait()
    copies[1].wait()
    for m in range(factor_out.shape[0]):
        factor_out[m] = jnp.full(factor_out.shape[1:], scale_s[kind_s[m]], jnp.float32)
    copies[2].wait()
    copies[3].wait()


def per_device(query, train, precond, module_kind, kind_scale):
    n, sections, halves = (lax.axis_size(a) for a in ("dp", "section", "half"))
    q_rows = query.shape[0]
    out_rows = n * q_rows // (sections * halves)
    direct = n <= DIRECT
    if direct:
        blocks = [query] + [lax.ppermute(query, "dp", [(i, (i + s) % n) for i in range(n)]) for s in range(1, n)]
    else:
        blocks = [lax.all_gather(query, "dp", axis=0, tiled=True)]
    mods, feat = precond.shape[:2]
    vmem, hbm = (pl.BlockSpec(memory_space=s) for s in (pltpu.VMEM, pltpu.HBM))
    staged = pl.pallas_call(
        stage,
        out_shape=(
            pltpu.VMEM(train.shape, train.dtype),
            pltpu.VMEM(precond.shape, precond.dtype),
            pltpu.VMEM((mods, 1, feat), jnp.float32),
        ),
        in_specs=[hbm] * 4,
        out_specs=(vmem,) * 3,
        scratch_shapes=[
            pltpu.SMEM(module_kind.shape, module_kind.dtype),
            pltpu.SMEM(kind_scale.shape, kind_scale.dtype),
            pltpu.SemaphoreType.DMA((4,)),
        ],
        cost_estimate=pl.CostEstimate(flops=0, bytes_accessed=2 * train.size * 2, transcendentals=0),
        compiler_params=pltpu.CompilerParams(vmem_limit_bytes=32 * 2**20),
        name="stage",
    )(*(pltpu.with_memory_space_constraint(a, pltpu.HBM) for a in (train, precond, module_kind, kind_scale)))
    part = jax.ShapeDtypeStruct((sections, out_rows, train.shape[0]), jnp.float32)
    keep, send = pl.pallas_call(
        functools.partial(local_scores, n, sections, halves, direct),
        out_shape=(part, part),
        in_specs=[vmem] * (len(blocks) + 3),
        out_specs=(vmem, vmem),
        compiler_params=pltpu.CompilerParams(vmem_limit_bytes=48 * 2**20),
        name="local_scores",
    )(*blocks, *staged)
    got = lax.ppermute(send, "half", [(i, 1 - i) for i in range(halves)])
    both = keep + got
    out = both[0]
    for s in range(1, sections):
        moved = lax.ppermute(both[s].astype(RT), "section", [(i, i ^ s) for i in range(sections)])
        out = out + moved.astype(jnp.float32)
    return out


RT = jnp.bfloat16


def solution(mesh):
    in_specs = (
        P("dp", SHARDS),
        P("dp", SHARDS),
        P(SHARDS, None, None),
        P(SHARDS),
        P(),
    )
    return jax.shard_map(
        per_device, mesh=mesh, in_specs=in_specs, out_specs=P(SHARDS, "dp"), check_vma=False
    )
```

```python
import functools

import jax
import jax.numpy as jnp
from jax import lax
from jax.experimental import pallas as pl
from jax.experimental.pallas import tpu as pltpu
from jax.sharding import PartitionSpec as P

SHARDS = ("section", "half")
DIRECT = 4
ROWS = 64
SHUFFLES = ((1, 3, 0, 2), (3, 2, 1, 0), (2, 0, 3, 1))
SENT = (1, 0, 2)
SECTION_ORDER = (1, 2, 3)


def stage(pieces, train, precond, kind, scale, train_t, precond_v, factor, raw, kind_s, scale_s, sems):
    rows = train.shape[0] // pieces
    cuts = [pl.ds(i * rows, rows) for i in range(pieces)]
    pairs = [(kind, kind_s), (scale, scale_s), (precond, precond_v)] + [(train.at[c], raw.at[c]) for c in cuts]
    copies = [pltpu.make_async_copy(src, dst, sems.at[i]) for i, (src, dst) in enumerate(pairs)]
    for c in copies:
        c.start()
    copies[0].wait()
    copies[1].wait()
    for m in range(factor.shape[0]):
        factor[m] = jnp.full(factor.shape[1:], scale_s[kind_s[m]], jnp.float32)
    for i in range(pieces):
        copies[3 + i].wait()
        train_t[:, i * rows:(i + 1) * rows] = raw[i * rows:(i + 1) * rows, :].T
    copies[2].wait()


def local_scores(n, sections, halves, direct, *refs):
    blocks, (train_t, precond, factor, kept, sent) = refs[:-5], refs[-5:]
    mods, feat = precond.shape[0], precond.shape[1]
    q_rows = blocks[0].shape[0] if direct else blocks[0].shape[0] // n
    own_rows = kept.shape[1]
    unit = min(q_rows, own_rows)
    dp, section, half = (lax.axis_index(a) for a in ("dp", "section", "half"))

    def work(lhs, rows, first_row):
        parts = []
        for m in range(mods):
            pre = jnp.dot(lhs(slice(m * feat, (m + 1) * feat)), precond[m], preferred_element_type=jnp.float32)
            parts.append((pre * factor[m]).astype(jnp.bfloat16))
        scores = jnp.dot(jnp.concatenate(parts, axis=1), train_t[...], preferred_element_type=jnp.float32)
        for i in range(rows // unit):
            row = first_row(i * unit)
            device, at = row // own_rows, pl.multiple_of(lax.rem(row, own_rows), unit)
            slot, mine = (device // halves) ^ section, lax.rem(device, halves) == half
            value = scores[i * unit:(i + 1) * unit]

            @pl.when(mine)
            def _():
                kept[slot, pl.ds(at, unit), :] = value

            @pl.when(jnp.logical_not(mine))
            def _():
                sent[slot, pl.ds(at, unit), :] = value.astype(sent.dtype)

    if direct:
        owners = [dp]
        for k in SENT:
            table = {t: i for i, t in enumerate(SHUFFLES[k])}
            owner = jnp.int32(table[0])
            for t in range(1, n):
                owner = jnp.where(dp == t, table[t], owner)
            owners.append(owner)
        work(lambda c: jnp.concatenate([b[:, c] for b in blocks], axis=0), n * q_rows, lambda r: owners[r // q_rows] * q_rows + r % q_rows)
    else:

        def step(c, carry):
            base = pl.multiple_of(c * ROWS, ROWS)
            work(lambda cols: blocks[0][pl.ds(base, ROWS), cols], ROWS, lambda r: base + r)
            return carry

        lax.fori_loop(0, n * q_rows // ROWS, step, 0)


def per_device(query, train, precond, module_kind, kind_scale):
    n, sections, halves = (lax.axis_size(a) for a in ("dp", "section", "half"))
    mods, feat = precond.shape[:2]
    cols, feats = train.shape
    own_rows = n * query.shape[0] // (sections * halves)
    direct = n == DIRECT
    if direct:
        blocks = [query] + [lax.ppermute(query, "dp", list(enumerate(SHUFFLES[k]))) for k in SENT]
    else:
        blocks = [lax.all_gather(query, "dp", axis=0, tiled=True)]

    vmem, hbm = (pl.BlockSpec(memory_space=s) for s in (pltpu.VMEM, pltpu.HBM))
    pieces = 4
    staged = pl.pallas_call(
        functools.partial(stage, pieces),
        out_shape=(
            pltpu.VMEM((feats, cols), train.dtype),
            pltpu.VMEM(precond.shape, precond.dtype),
            pltpu.VMEM((mods, 1, feat), jnp.float32),
        ),
        in_specs=[hbm] * 4,
        out_specs=(vmem,) * 3,
        scratch_shapes=[
            pltpu.VMEM(train.shape, train.dtype),
            pltpu.SMEM(module_kind.shape, module_kind.dtype),
            pltpu.SMEM(kind_scale.shape, kind_scale.dtype),
            pltpu.SemaphoreType.DMA((3 + pieces,)),
        ],
        cost_estimate=pl.CostEstimate(flops=0, bytes_accessed=4 * train.size, transcendentals=0),
        compiler_params=pltpu.CompilerParams(vmem_limit_bytes=32 * 2**20),
        name="stage",
    )(*(pltpu.with_memory_space_constraint(a, pltpu.HBM) for a in (train, precond, module_kind, kind_scale)))
    shape = (sections, own_rows, cols)
    kept, sent = pl.pallas_call(
        functools.partial(local_scores, n, sections, halves, direct),
        out_shape=(jax.ShapeDtypeStruct(shape, jnp.float32), jax.ShapeDtypeStruct(shape, jnp.float32)),
        in_specs=[vmem] * (len(blocks) + 3),
        out_specs=(vmem, vmem),
        compiler_params=pltpu.CompilerParams(vmem_limit_bytes=48 * 2**20),
        name="local_scores",
    )(*blocks, *staged)

    got = lax.ppermute(sent, "half", [(i, halves - 1 - i) for i in range(halves)])
    total = kept + got.astype(jnp.float32)
    out = total[0]
    for s in SECTION_ORDER if sections == 4 else range(1, sections):
        moved = lax.ppermute(total[s].astype(jnp.bfloat16), "section", [(i, i ^ s) for i in range(sections)])
        out = out + moved.astype(jnp.float32)
    return out


def solution(mesh):
    in_specs = (
        P("dp", SHARDS),
        P("dp", SHARDS),
        P(SHARDS, None, None),
        P(SHARDS),
        P(),
    )
    return jax.shard_map(
        per_device, mesh=mesh, in_specs=in_specs, out_specs=P(SHARDS, "dp"), check_vma=False
    )
```

```python
import functools

import jax
import jax.numpy as jnp
from jax import lax
from jax.experimental import pallas as pl
from jax.experimental.pallas import tpu as pltpu
from jax.sharding import PartitionSpec as P

SHARDS = ("section", "half")
DIRECT = 4
ROWS = 64
SHUFFLES = ((2, 3, 1, 0), (3, 2, 0, 1), (1, 0, 3, 2))
NEAR = (1, 3)


def stage(pieces, train, precond, kind, scale, train_t, precond_v, factor, raw, kind_s, scale_s, sems):
    rows = train.shape[0] // pieces
    cuts = [pl.ds(i * rows, rows) for i in range(pieces)]
    pairs = [(kind, kind_s), (scale, scale_s), (precond, precond_v)] + [(train.at[c], raw.at[c]) for c in cuts]
    copies = [pltpu.make_async_copy(src, dst, sems.at[i]) for i, (src, dst) in enumerate(pairs)]
    for c in copies:
        c.start()
    copies[0].wait()
    copies[1].wait()
    for m in range(factor.shape[0]):
        factor[m] = jnp.full(factor.shape[1:], scale_s[kind_s[m]], jnp.float32)
    for i in range(pieces):
        copies[3 + i].wait()
        train_t[:, i * rows:(i + 1) * rows] = raw[i * rows:(i + 1) * rows, :].T
    copies[2].wait()


def local_scores(n, direct, *refs, far):
    blocks, (train_t, precond, factor), outs = refs[:-6 - len(far)], refs[-6 - len(far):-3 - len(far)], refs[-3 - len(far):]
    own, near, swap, aways = outs[0], outs[1], outs[2], outs[3:]
    mods, feat = precond.shape[0], precond.shape[1]
    q_rows = blocks[0].shape[0] if direct else blocks[0].shape[0] // n
    own_rows = own.shape[0]
    unit = min(q_rows, own_rows)
    dp, section, half = (lax.axis_index(a) for a in ("dp", "section", "half"))
    routes = [(0, own), (jnp.where(half == 0, *NEAR), near), (jnp.where(half == 0, *NEAR[::-1]), swap)] + list(zip(far, aways))

    def work(lhs, rows, first_row):
        parts = []
        for m in range(mods):
            pre = jnp.dot(lhs(slice(m * feat, (m + 1) * feat)), precond[m], preferred_element_type=jnp.float32)
            parts.append((pre * factor[m]).astype(jnp.bfloat16))
        scores = jnp.dot(jnp.concatenate(parts, axis=1), train_t[...], preferred_element_type=jnp.float32)
        for i in range(rows // unit):
            row = first_row(i * unit)
            away, at = (row // own_rows) ^ section, pl.multiple_of(lax.rem(row, own_rows), unit)
            value = scores[i * unit:(i + 1) * unit]
            for distance, out in routes:

                @pl.when(away == distance)
                def _(out=out):
                    out[pl.ds(at, unit), :] = value.astype(out.dtype)

    if direct:
        owners = [dp]
        for shuffle in SHUFFLES:
            owners.append(sum(jnp.where(dp == target, source, 0) for source, target in enumerate(shuffle)))
        work(lambda c: jnp.concatenate([b[:, c] for b in blocks], axis=0), n * q_rows, lambda r: owners[r // q_rows] * q_rows + r % q_rows)
    else:

        def step(c, carry):
            base = pl.multiple_of(c * ROWS, ROWS)
            work(lambda cols: blocks[0][pl.ds(base, ROWS), cols], ROWS, lambda r: base + r)
            return carry

        lax.fori_loop(0, n * q_rows // ROWS, step, 0)


def per_device(query, train, precond, module_kind, kind_scale):
    n, sections = lax.axis_size("dp"), lax.axis_size("section")
    mods, feat = precond.shape[:2]
    cols, feats = train.shape
    own_rows = n * query.shape[0] // sections
    direct = n == DIRECT
    if direct:
        blocks = [query] + [lax.ppermute(query, "dp", list(enumerate(s))) for s in SHUFFLES]
    else:
        blocks = [lax.all_gather(query, "dp", axis=0, tiled=True)]

    vmem, hbm = (pl.BlockSpec(memory_space=s) for s in (pltpu.VMEM, pltpu.HBM))
    pieces = 4
    staged = pl.pallas_call(
        functools.partial(stage, pieces),
        out_shape=(
            pltpu.VMEM((feats, cols), train.dtype),
            pltpu.VMEM(precond.shape, precond.dtype),
            pltpu.VMEM((mods, 1, feat), jnp.float32),
        ),
        in_specs=[hbm] * 4,
        out_specs=(vmem,) * 3,
        scratch_shapes=[
            pltpu.VMEM(train.shape, train.dtype),
            pltpu.SMEM(module_kind.shape, module_kind.dtype),
            pltpu.SMEM(kind_scale.shape, kind_scale.dtype),
            pltpu.SemaphoreType.DMA((3 + pieces,)),
        ],
        cost_estimate=pl.CostEstimate(flops=0, bytes_accessed=4 * train.size, transcendentals=0),
        compiler_params=pltpu.CompilerParams(vmem_limit_bytes=32 * 2**20),
        name="stage",
    )(*(pltpu.with_memory_space_constraint(a, pltpu.HBM) for a in (train, precond, module_kind, kind_scale)))
    far = tuple(s for s in range(1, sections) if s not in NEAR)
    shape = (own_rows, cols)
    whole, half_width = jax.ShapeDtypeStruct(shape, jnp.float32), jax.ShapeDtypeStruct(shape, jnp.bfloat16)
    own, near, swap, *aways = pl.pallas_call(
        functools.partial(local_scores, n, direct, far=far),
        out_shape=(whole, whole, whole) + (half_width,) * len(far),
        in_specs=[vmem] * (len(blocks) + 3),
        out_specs=(vmem,) * (3 + len(far)),
        compiler_params=pltpu.CompilerParams(vmem_limit_bytes=48 * 2**20),
        name="local_scores",
    )(*blocks, *staged)

    def across(x):
        return lax.ppermute(x, "half", [(0, 1), (1, 0)])

    near = (near + across(swap)).astype(jnp.bfloat16)
    for s, away in zip(far, aways):
        own = own + lax.ppermute(away, "section", [(i, i ^ s) for i in range(sections)]).astype(jnp.float32)
    pairs = [(2 * i + h, 2 * (i ^ NEAR[h]) + h) for i in range(sections) for h in range(2)]
    own = own + lax.ppermute(near, SHARDS, pairs).astype(jnp.float32)
    rows = own_rows // 2
    first = lax.axis_index("half") == 0
    mine = jnp.where(first, own[:rows], own[rows:])
    return mine + across(jnp.where(first, own[rows:], own[:rows]))


def solution(mesh):
    in_specs = (
        P("dp", SHARDS),
        P("dp", SHARDS),
        P(SHARDS, None, None),
        P(SHARDS),
        P(),
    )
    return jax.shard_map(
        per_device, mesh=mesh, in_specs=in_specs, out_specs=P(SHARDS, "dp"), check_vma=False
    )
```

```python
import functools

import jax
import jax.numpy as jnp
from jax import lax
from jax.experimental import pallas as pl
from jax.experimental.pallas import tpu as pltpu
from jax.sharding import PartitionSpec as P

SHARDS = ("section", "half")
DIRECT = 4
ROWS = 64
SHUFFLES = ((1, 3, 2, 0), (2, 1, 0, 3), (3, 0, 1, 2), (0, 2, 3, 1))
NEAR = (1, 3)


def stage(pieces, train, precond, kind, scale, train_t, precond_v, factor, raw, kind_s, scale_s, sems):
    rows = train.shape[0] // pieces
    cuts = [pl.ds(i * rows, rows) for i in range(pieces)]
    pairs = [(kind, kind_s), (scale, scale_s), (precond, precond_v)] + [(train.at[c], raw.at[c]) for c in cuts]
    copies = [pltpu.make_async_copy(src, dst, sems.at[i]) for i, (src, dst) in enumerate(pairs)]
    for c in copies:
        c.start()
    copies[0].wait()
    copies[1].wait()
    for m in range(factor.shape[0]):
        factor[m] = jnp.full(factor.shape[1:], scale_s[kind_s[m]], jnp.float32)
    for i in range(pieces):
        copies[3 + i].wait()
        train_t[:, i * rows:(i + 1) * rows] = raw[i * rows:(i + 1) * rows, :].T
    copies[2].wait()


def local_scores(n, blocks_in, *refs, far):
    blocks, (train_t, precond, factor, own, near, swap, *aways), queries = refs[:blocks_in], refs[blocks_in:-1], refs[-1]
    mods, feat = precond.shape[0], precond.shape[1]
    q_rows = queries.shape[0] // n
    own_rows = own.shape[0]
    unit = min(q_rows, own_rows)
    dp, section, half = (lax.axis_index(a) for a in ("dp", "section", "half"))
    routes = [(0, own), (jnp.where(half == 0, *NEAR), near), (jnp.where(half == 0, *NEAR[::-1]), swap)] + list(zip(far, aways))

    def work(lhs, rows, first):
        parts = []
        for m in range(mods):
            pre = jnp.dot(lhs[:, m * feat:(m + 1) * feat], precond[m], preferred_element_type=jnp.float32)
            parts.append((pre * factor[m]).astype(jnp.bfloat16))
        scores = jnp.dot(jnp.concatenate(parts, axis=1), train_t[...], preferred_element_type=jnp.float32)
        for i in range(rows // unit):
            row = first + i * unit
            away, at = (row // own_rows) ^ section, pl.multiple_of(lax.rem(row, own_rows), unit)
            value = scores[i * unit:(i + 1) * unit]
            for distance, out in routes:

                @pl.when(away == distance)
                def _(out=out):
                    out[pl.ds(at, unit), :] = value.astype(out.dtype)

    if blocks_in > 1:
        for shuffle, block in zip(SHUFFLES, blocks[1:]):
            owner = sum(jnp.where(dp == target, source, 0) for source, target in enumerate(shuffle))
            queries[pl.ds(pl.multiple_of(owner * q_rows, q_rows), q_rows), :] = block[...]
        queries[pl.ds(pl.multiple_of(dp * q_rows, q_rows), q_rows), :] = blocks[0][...]
        work(queries, n * q_rows, 0)
    else:

        def step(c, carry):
            base = pl.multiple_of(c * ROWS, ROWS)
            work(blocks[0].at[pl.ds(base, ROWS)], ROWS, base)
            return carry

        lax.fori_loop(0, n * q_rows // ROWS, step, 0)


def per_device(query, train, precond, module_kind, kind_scale):
    n, sections = lax.axis_size("dp"), lax.axis_size("section")
    mods, feat = precond.shape[:2]
    cols, feats = train.shape
    own_rows = n * query.shape[0] // sections
    direct = n == DIRECT
    if direct:
        blocks = [query] + [
            lax.ppermute(query, ("half", "dp"), [(n * h + i, n * (h if i != t else 1 - h) + t) for h in range(2) for i, t in enumerate(s)])
            for s in SHUFFLES
        ]
    else:
        blocks = [lax.all_gather(query, "dp", axis=0, tiled=True)]

    vmem, hbm = (pl.BlockSpec(memory_space=s) for s in (pltpu.VMEM, pltpu.HBM))
    pieces = 4
    staged = pl.pallas_call(
        functools.partial(stage, pieces),
        out_shape=(
            pltpu.VMEM((feats, cols), train.dtype),
            pltpu.VMEM(precond.shape, precond.dtype),
            pltpu.VMEM((mods, 1, feat), jnp.float32),
        ),
        in_specs=[hbm] * 4,
        out_specs=(vmem,) * 3,
        scratch_shapes=[
            pltpu.VMEM(train.shape, train.dtype),
            pltpu.SMEM(module_kind.shape, module_kind.dtype),
            pltpu.SMEM(kind_scale.shape, kind_scale.dtype),
            pltpu.SemaphoreType.DMA((3 + pieces,)),
        ],
        cost_estimate=pl.CostEstimate(flops=0, bytes_accessed=4 * train.size, transcendentals=0),
        compiler_params=pltpu.CompilerParams(vmem_limit_bytes=32 * 2**20),
        name="stage",
    )(*(pltpu.with_memory_space_constraint(a, pltpu.HBM) for a in (train, precond, module_kind, kind_scale)))
    far = tuple(s for s in range(1, sections) if s not in NEAR)
    shape = (own_rows, cols)
    whole, half_width = jax.ShapeDtypeStruct(shape, jnp.float32), jax.ShapeDtypeStruct(shape, jnp.bfloat16)
    own, near, swap, *aways = pl.pallas_call(
        functools.partial(local_scores, n, len(blocks), far=far),
        out_shape=(whole, whole, whole) + (half_width,) * len(far),
        in_specs=[vmem] * (len(blocks) + 3),
        out_specs=(vmem,) * (3 + len(far)),
        scratch_shapes=[pltpu.VMEM((n * query.shape[0], feats), query.dtype)],
        compiler_params=pltpu.CompilerParams(vmem_limit_bytes=48 * 2**20),
        name="local_scores",
    )(*blocks, *staged)

    def across(x):
        return lax.ppermute(x, "half", [(0, 1), (1, 0)])

    near = (near + across(swap)).astype(jnp.bfloat16)
    for s, away in zip(far, aways):
        own = own + lax.ppermute(away, "section", [(i, i ^ s) for i in range(sections)]).astype(jnp.float32)
    pairs = [(2 * i + h, 2 * (i ^ NEAR[h]) + h) for i in range(sections) for h in range(2)]
    own = own + lax.ppermute(near, SHARDS, pairs).astype(jnp.float32)
    rows = own_rows // 2
    first = lax.axis_index("half") == 0
    mine = jnp.where(first, own[:rows], own[rows:])
    return mine + across(jnp.where(first, own[rows:], own[:rows]))


def solution(mesh):
    in_specs = (
        P("dp", SHARDS),
        P("dp", SHARDS),
        P(SHARDS, None, None),
        P(SHARDS),
        P(),
    )
    return jax.shard_map(
        per_device, mesh=mesh, in_specs=in_specs, out_specs=P(SHARDS, "dp"), check_vma=False
    )
```

```python
import functools

import jax
import jax.numpy as jnp
from jax import lax
from jax.experimental import pallas as pl
from jax.experimental.pallas import tpu as pltpu
from jax.sharding import PartitionSpec as P

SHARDS = ("section", "half")
DIRECT = 4
ROWS = 64
SHUFFLES = ((1, 3, 2, 0), (2, 1, 0, 3), (3, 0, 1, 2), (0, 2, 3, 1))
NEAR = (1, 3)


def stage(pieces, train, precond, kind, scale, train_t, precond_v, factor, raw, kind_s, scale_s, sems):
    rows = train.shape[0] // pieces
    cuts = [pl.ds(i * rows, rows) for i in range(pieces)]
    pairs = [(kind, kind_s), (scale, scale_s), (precond, precond_v)] + [(train.at[c], raw.at[c]) for c in cuts]
    copies = [pltpu.make_async_copy(src, dst, sems.at[i]) for i, (src, dst) in enumerate(pairs)]
    for c in copies:
        c.start()
    copies[0].wait()
    copies[1].wait()
    for m in range(factor.shape[0]):
        factor[m] = jnp.full(factor.shape[1:], scale_s[kind_s[m]], jnp.float32)
    for i in range(pieces):
        copies[3 + i].wait()
        train_t[:, i * rows:(i + 1) * rows] = raw[i * rows:(i + 1) * rows, :].T
    copies[2].wait()


def weighted_scores(lhs, train_t, precond, factor):
    mods, feat = precond.shape[0], precond.shape[1]
    parts = []
    for m in range(mods):
        pre = jnp.dot(lhs[:, m * feat:(m + 1) * feat], precond[m], preferred_element_type=jnp.float32)
        parts.append((pre * factor[m]).astype(jnp.bfloat16))
    return jnp.dot(jnp.concatenate(parts, axis=1), train_t[...], preferred_element_type=jnp.float32)


def local_scores(n, blocks_in, far, *refs):
    blocks, (train_t, precond, factor, *outs), queries = refs[:blocks_in], refs[blocks_in:-1], refs[-1]
    q_rows = queries.shape[0] // n
    own_rows = outs[0].shape[0]
    dp, section, half = (lax.axis_index(a) for a in ("dp", "section", "half"))
    served = jnp.where(half == 0, *NEAR)
    distances = (0, served, sum(NEAR) - served) + far

    if blocks_in > 1:

        def put(owner, block):
            away = owner ^ section
            place = sum(jnp.where(away == distance, i, 0) for i, distance in enumerate(distances))
            queries[pl.ds(pl.multiple_of(place * q_rows, q_rows), q_rows), :] = block[...]

        for shuffle, block in zip(SHUFFLES, blocks[1:]):
            put(sum(jnp.where(dp == target, source, 0) for source, target in enumerate(shuffle)), block)
        put(dp, blocks[0])
        scores = weighted_scores(queries, train_t, precond, factor)
        for i, out in enumerate(outs):
            out[...] = scores[i * own_rows:(i + 1) * own_rows].astype(out.dtype)
    else:
        unit = min(q_rows, own_rows)

        def step(c, carry):
            base = pl.multiple_of(c * ROWS, ROWS)
            scores = weighted_scores(blocks[0].at[pl.ds(base, ROWS)], train_t, precond, factor)
            for i in range(ROWS // unit):
                row = base + i * unit
                away, at = (row // own_rows) ^ section, pl.multiple_of(lax.rem(row, own_rows), unit)
                for distance, out in zip(distances, outs):

                    @pl.when(away == distance)
                    def _(i=i, at=at, out=out):
                        out[pl.ds(at, unit), :] = scores[i * unit:(i + 1) * unit].astype(out.dtype)

            return carry

        lax.fori_loop(0, n * q_rows // ROWS, step, 0)


def per_device(query, train, precond, module_kind, kind_scale):
    n, sections = lax.axis_size("dp"), lax.axis_size("section")
    mods, feat = precond.shape[:2]
    cols, feats = train.shape
    own_rows = n * query.shape[0] // sections
    direct = n == sections == DIRECT
    if direct:
        blocks = [query] + [
            lax.ppermute(query, ("half", "dp"), [(n * h + i, n * (h if i != t else 1 - h) + t) for h in range(2) for i, t in enumerate(s)])
            for s in SHUFFLES
        ]
    else:
        blocks = [lax.all_gather(query, "dp", axis=0, tiled=True)]

    vmem, hbm = (pl.BlockSpec(memory_space=s) for s in (pltpu.VMEM, pltpu.HBM))
    pieces = 4
    staged = pl.pallas_call(
        functools.partial(stage, pieces),
        out_shape=(
            pltpu.VMEM((feats, cols), train.dtype),
            pltpu.VMEM(precond.shape, precond.dtype),
            pltpu.VMEM((mods, 1, feat), jnp.float32),
        ),
        in_specs=[hbm] * 4,
        out_specs=(vmem,) * 3,
        scratch_shapes=[
            pltpu.VMEM(train.shape, train.dtype),
            pltpu.SMEM(module_kind.shape, module_kind.dtype),
            pltpu.SMEM(kind_scale.shape, kind_scale.dtype),
            pltpu.SemaphoreType.DMA((3 + pieces,)),
        ],
        cost_estimate=pl.CostEstimate(flops=0, bytes_accessed=4 * train.size, transcendentals=0),
        compiler_params=pltpu.CompilerParams(vmem_limit_bytes=32 * 2**20),
        name="stage",
    )(*(pltpu.with_memory_space_constraint(a, pltpu.HBM) for a in (train, precond, module_kind, kind_scale)))
    far = tuple(s for s in range(1, sections) if s not in NEAR)
    shape = (own_rows, cols)
    whole, half_width = jax.ShapeDtypeStruct(shape, jnp.float32), jax.ShapeDtypeStruct(shape, jnp.bfloat16)
    own, near, swap, *aways = pl.pallas_call(
        functools.partial(local_scores, n, len(blocks), far),
        out_shape=(whole, whole, whole) + (half_width,) * len(far),
        in_specs=[vmem] * (len(blocks) + 3),
        out_specs=(vmem,) * (3 + len(far)),
        scratch_shapes=[pltpu.VMEM((n * query.shape[0], feats), query.dtype)],
        compiler_params=pltpu.CompilerParams(vmem_limit_bytes=48 * 2**20),
        name="local_scores",
    )(*blocks, *staged)

    def across(x):
        return lax.ppermute(x, "half", [(0, 1), (1, 0)])

    near = (near + across(swap)).astype(jnp.bfloat16)
    for s, away in zip(far, aways):
        own = own + lax.ppermute(away, "section", [(i, i ^ s) for i in range(sections)]).astype(jnp.float32)
    pairs = [(2 * i + h, 2 * (i ^ NEAR[h]) + h) for i in range(sections) for h in range(2)]
    own = own + lax.ppermute(near, SHARDS, pairs).astype(jnp.float32)
    rows = own_rows // 2
    first = lax.axis_index("half") == 0
    mine = jnp.where(first, own[:rows], own[rows:])
    return mine + across(jnp.where(first, own[rows:], own[:rows]))


def solution(mesh):
    in_specs = (
        P("dp", SHARDS),
        P("dp", SHARDS),
        P(SHARDS, None, None),
        P(SHARDS),
        P(),
    )
    return jax.shard_map(
        per_device, mesh=mesh, in_specs=in_specs, out_specs=P(SHARDS, "dp"), check_vma=False
    )
```

```python
import functools

import jax
import jax.numpy as jnp
from jax import lax
from jax.experimental import pallas as pl
from jax.experimental.pallas import tpu as pltpu
from jax.sharding import PartitionSpec as P

SHARDS = ("section", "half")
DIRECT = 4
ROWS = 64
SHUFFLES = ((1, 3, 2, 0), (2, 1, 0, 3), (3, 0, 1, 2), (0, 2, 3, 1))
ROUTES = ((2, 3, 0, 1), (3, 0, 1, 2), (1, 2, 3, 0))


def stage(pieces, train, precond, kind, scale, train_t, precond_v, factor, raw, kind_s, scale_s, sems):
    rows = train.shape[0] // pieces
    cuts = [pl.ds(i * rows, rows) for i in range(pieces)]
    pairs = [(kind, kind_s), (scale, scale_s), (precond, precond_v)] + [(train.at[c], raw.at[c]) for c in cuts]
    copies = [pltpu.make_async_copy(src, dst, sems.at[i]) for i, (src, dst) in enumerate(pairs)]
    for c in copies:
        c.start()
    copies[0].wait()
    copies[1].wait()
    for m in range(factor.shape[0]):
        factor[m] = jnp.full(factor.shape[1:], scale_s[kind_s[m]], jnp.float32)
    for i in range(pieces):
        copies[3 + i].wait()
        train_t[:, i * rows:(i + 1) * rows] = raw[i * rows:(i + 1) * rows, :].T
    copies[2].wait()


def weighted_scores(lhs, train_t, precond, factor):
    mods, feat = precond.shape[0], precond.shape[1]
    parts = []
    for m in range(mods):
        pre = jnp.dot(lhs[:, m * feat:(m + 1) * feat], precond[m], preferred_element_type=jnp.float32)
        parts.append((pre * factor[m]).astype(jnp.bfloat16))
    return jnp.dot(jnp.concatenate(parts, axis=1), train_t[...], preferred_element_type=jnp.float32)


def local_scores(n, blocks_in, routes, *refs):
    blocks, (train_t, precond, factor, *outs), queries = refs[:blocks_in], refs[blocks_in:-1], refs[-1]
    q_rows = queries.shape[0] // n
    own_rows = outs[0].shape[0]
    dp, section, half = (lax.axis_index(a) for a in ("dp", "section", "half"))
    to = [sum(jnp.where(section == source, target, 0) for source, target in enumerate(route)) for route in routes]
    homes = (section, jnp.where(half == 0, to[0], to[1]), jnp.where(half == 0, to[1], to[0]), *to[2:])

    if blocks_in > 1:

        def put(owner, block):
            place = sum(jnp.where(owner == home, i, 0) for i, home in enumerate(homes))
            queries[pl.ds(pl.multiple_of(place * q_rows, q_rows), q_rows), :] = block[...]

        for shuffle, block in zip(SHUFFLES, blocks[1:]):
            put(sum(jnp.where(dp == target, source, 0) for source, target in enumerate(shuffle)), block)
        put(dp, blocks[0])
        scores = weighted_scores(queries, train_t, precond, factor)
        for i, out in enumerate(outs):
            out[...] = scores[i * own_rows:(i + 1) * own_rows].astype(out.dtype)
    else:
        unit = min(q_rows, own_rows)

        def step(c, carry):
            base = pl.multiple_of(c * ROWS, ROWS)
            scores = weighted_scores(blocks[0].at[pl.ds(base, ROWS)], train_t, precond, factor)
            for i in range(ROWS // unit):
                row = base + i * unit
                at = pl.multiple_of(lax.rem(row, own_rows), unit)
                for home, out in zip(homes, outs):

                    @pl.when(row // own_rows == home)
                    def _(i=i, at=at, out=out):
                        out[pl.ds(at, unit), :] = scores[i * unit:(i + 1) * unit].astype(out.dtype)

            return carry

        lax.fori_loop(0, n * q_rows // ROWS, step, 0)


def per_device(query, train, precond, module_kind, kind_scale):
    n, sections = lax.axis_size("dp"), lax.axis_size("section")
    mods, feat = precond.shape[:2]
    cols, feats = train.shape
    own_rows = n * query.shape[0] // sections
    direct = n == sections == DIRECT
    if direct:
        blocks = [query] + [
            lax.ppermute(query, ("half", "dp"), [(n * h + i, n * (h if i != t else 1 - h) + t) for h in range(2) for i, t in enumerate(s)])
            for s in SHUFFLES
        ]
    else:
        blocks = [lax.all_gather(query, "dp", axis=0, tiled=True)]

    vmem, hbm = (pl.BlockSpec(memory_space=s) for s in (pltpu.VMEM, pltpu.HBM))
    pieces = 4
    staged = pl.pallas_call(
        functools.partial(stage, pieces),
        out_shape=(
            pltpu.VMEM((feats, cols), train.dtype),
            pltpu.VMEM(precond.shape, precond.dtype),
            pltpu.VMEM((mods, 1, feat), jnp.float32),
        ),
        in_specs=[hbm] * 4,
        out_specs=(vmem,) * 3,
        scratch_shapes=[
            pltpu.VMEM(train.shape, train.dtype),
            pltpu.SMEM(module_kind.shape, module_kind.dtype),
            pltpu.SMEM(kind_scale.shape, kind_scale.dtype),
            pltpu.SemaphoreType.DMA((3 + pieces,)),
        ],
        cost_estimate=pl.CostEstimate(flops=0, bytes_accessed=4 * train.size, transcendentals=0),
        compiler_params=pltpu.CompilerParams(vmem_limit_bytes=32 * 2**20),
        name="stage",
    )(*(pltpu.with_memory_space_constraint(a, pltpu.HBM) for a in (train, precond, module_kind, kind_scale)))
    routes = ROUTES if sections == 4 else tuple(tuple(i ^ s for i in range(sections)) for s in range(1, sections))
    far = routes[2:]
    shape = (own_rows, cols)
    whole, half_width = jax.ShapeDtypeStruct(shape, jnp.float32), jax.ShapeDtypeStruct(shape, jnp.bfloat16)
    own, near, swap, *aways = pl.pallas_call(
        functools.partial(local_scores, n, len(blocks), routes),
        out_shape=(whole, whole, whole) + (half_width,) * len(far),
        in_specs=[vmem] * (len(blocks) + 3),
        out_specs=(vmem,) * (3 + len(far)),
        scratch_shapes=[pltpu.VMEM((n * query.shape[0], feats), query.dtype)],
        compiler_params=pltpu.CompilerParams(vmem_limit_bytes=48 * 2**20),
        name="local_scores",
    )(*blocks, *staged)

    def across(x):
        return lax.ppermute(x, "half", [(0, 1), (1, 0)])

    near = (near + across(swap)).astype(jnp.bfloat16)
    for route, away in zip(far, aways):
        own = own + lax.ppermute(away, "section", list(enumerate(route))).astype(jnp.float32)
    pairs = [(2 * i + h, 2 * routes[h][i] + 1 - h) for i in range(sections) for h in range(2)]
    own = own + lax.ppermute(near, SHARDS, pairs).astype(jnp.float32)
    rows = own_rows // 2
    first = lax.axis_index("half") == 0
    mine = jnp.where(first, own[:rows], own[rows:])
    return mine + across(jnp.where(first, own[rows:], own[:rows]))


def solution(mesh):
    in_specs = (
        P("dp", SHARDS),
        P("dp", SHARDS),
        P(SHARDS, None, None),
        P(SHARDS),
        P(),
    )
    return jax.shard_map(
        per_device, mesh=mesh, in_specs=in_specs, out_specs=P(SHARDS, "dp"), check_vma=False
    )
```

```python
import functools

import jax
import jax.numpy as jnp
from jax import lax
from jax.experimental import pallas as pl
from jax.experimental.pallas import tpu as pltpu
from jax.sharding import PartitionSpec as P

SHARDS = ("section", "half")
DIRECT = 4
EARLY = 2
ROWS = 64
SHUFFLES = ((1, 3, 2, 0), (2, 1, 0, 3), (3, 0, 1, 2), (0, 2, 3, 1))
ROUTES = ((3, 2, 0, 1), (1, 0, 3, 2), (2, 3, 1, 0))


def stage(pieces, train, precond, kind, scale, train_t, precond_v, factor, raw, kind_s, scale_s, sems):
    rows = train.shape[0] // pieces
    cuts = [pl.ds(i * rows, rows) for i in range(pieces)]
    pairs = [(kind, kind_s), (scale, scale_s), (precond, precond_v)] + [(train.at[c], raw.at[c]) for c in cuts]
    copies = [pltpu.make_async_copy(src, dst, sems.at[i]) for i, (src, dst) in enumerate(pairs)]
    for c in copies:
        c.start()
    copies[0].wait()
    copies[1].wait()
    for m in range(factor.shape[0]):
        factor[m] = jnp.full(factor.shape[1:], scale_s[kind_s[m]], jnp.float32)
    for i in range(pieces):
        copies[3 + i].wait()
        train_t[:, i * rows:(i + 1) * rows] = raw[i * rows:(i + 1) * rows, :].T
    copies[2].wait()


def weighted_scores(lhs, train_t, precond, factor):
    mods, feat = precond.shape[0], precond.shape[1]
    parts = []
    for m in range(mods):
        pre = jnp.dot(lhs[:, m * feat:(m + 1) * feat], precond[m], preferred_element_type=jnp.float32)
        parts.append((pre * factor[m]).astype(jnp.bfloat16))
    return jnp.dot(jnp.concatenate(parts, axis=1), train_t[...], preferred_element_type=jnp.float32)


def destinations(routes):
    section, half = lax.axis_index("section"), lax.axis_index("half")
    to = [sum(jnp.where(section == source, target, 0) for source, target in enumerate(route)) for route in routes]
    return (section, jnp.where(half == 0, to[0], to[1]), jnp.where(half == 0, to[1], to[0]), *to[2:])


def sender(shuffle):
    dp = lax.axis_index("dp")
    return sum(jnp.where(dp == target, source, 0) for source, target in enumerate(shuffle))


def early_scores(routes, *refs):
    blocks, (train_t, precond, factor, out) = refs[:1 + EARLY], refs[1 + EARLY:]
    homes, rows = destinations(routes), blocks[0].shape[0]
    scores = weighted_scores(jnp.concatenate([b[...] for b in blocks], axis=0), train_t, precond, factor)
    owners = [lax.axis_index("dp")] + [sender(s) for s in SHUFFLES[:EARLY]]
    for i in reversed(range(1 + EARLY)):
        place = sum(jnp.where(owners[i] == home, k, 0) for k, home in enumerate(homes))
        out[place] = scores[i * rows:(i + 1) * rows]


def late_scores(routes, *refs):
    count = len(SHUFFLES) - EARLY
    blocks, (train_t, precond, factor, early, out) = refs[:count], refs[count:]
    homes, rows, dp = destinations(routes), blocks[0].shape[0], lax.axis_index("dp")
    owners = [sender(s) for s in SHUFFLES[EARLY:]]

    def add(used):
        scores = weighted_scores(jnp.concatenate([b[...] for b in blocks[:used]], axis=0), train_t, precond, factor)
        for i in range(used):
            place = sum(jnp.where(owners[i] == home, k, 0) for k, home in enumerate(homes))
            out[place] = scores[i * rows:(i + 1) * rows]

    out[...] = early[...]
    idle = owners[-1] == dp
    pl.when(idle)(lambda: add(count - 1))
    pl.when(jnp.logical_not(idle))(lambda: add(count))


def local_scores(n, blocks_in, routes, *refs):
    blocks, (train_t, precond, factor, *outs), queries = refs[:blocks_in], refs[blocks_in:-1], refs[-1]
    q_rows = queries.shape[0] // n
    own_rows = outs[0].shape[0]
    dp, section, half = (lax.axis_index(a) for a in ("dp", "section", "half"))
    to = [sum(jnp.where(section == source, target, 0) for source, target in enumerate(route)) for route in routes]
    homes = (section, jnp.where(half == 0, to[0], to[1]), jnp.where(half == 0, to[1], to[0]), *to[2:])

    if blocks_in > 1:

        def put(owner, block):
            place = sum(jnp.where(owner == home, i, 0) for i, home in enumerate(homes))
            queries[pl.ds(pl.multiple_of(place * q_rows, q_rows), q_rows), :] = block[...]

        for shuffle, block in zip(SHUFFLES, blocks[1:]):
            put(sum(jnp.where(dp == target, source, 0) for source, target in enumerate(shuffle)), block)
        put(dp, blocks[0])
        scores = weighted_scores(queries, train_t, precond, factor)
        for i, out in enumerate(outs):
            out[...] = scores[i * own_rows:(i + 1) * own_rows].astype(out.dtype)
    else:
        unit = min(q_rows, own_rows)

        def step(c, carry):
            base = pl.multiple_of(c * ROWS, ROWS)
            scores = weighted_scores(blocks[0].at[pl.ds(base, ROWS)], train_t, precond, factor)
            for i in range(ROWS // unit):
                row = base + i * unit
                at = pl.multiple_of(lax.rem(row, own_rows), unit)
                for home, out in zip(homes, outs):

                    @pl.when(row // own_rows == home)
                    def _(i=i, at=at, out=out):
                        out[pl.ds(at, unit), :] = scores[i * unit:(i + 1) * unit].astype(out.dtype)

            return carry

        lax.fori_loop(0, n * q_rows // ROWS, step, 0)


def per_device(query, train, precond, module_kind, kind_scale):
    n, sections = lax.axis_size("dp"), lax.axis_size("section")
    mods, feat = precond.shape[:2]
    cols, feats = train.shape
    own_rows = n * query.shape[0] // sections
    direct = n == sections == DIRECT
    if direct:
        blocks = [query] + [
            lax.ppermute(query, ("half", "dp"), [(n * h + i, n * (h if i != t else 1 - h) + t) for h in range(2) for i, t in enumerate(s)])
            for s in SHUFFLES
        ]
    else:
        blocks = [lax.all_gather(query, "dp", axis=0, tiled=True)]

    vmem, hbm = (pl.BlockSpec(memory_space=s) for s in (pltpu.VMEM, pltpu.HBM))
    pieces = 4
    staged = pl.pallas_call(
        functools.partial(stage, pieces),
        out_shape=(
            pltpu.VMEM((feats, cols), train.dtype),
            pltpu.VMEM(precond.shape, precond.dtype),
            pltpu.VMEM((mods, 1, feat), jnp.float32),
        ),
        in_specs=[hbm] * 4,
        out_specs=(vmem,) * 3,
        scratch_shapes=[
            pltpu.VMEM(train.shape, train.dtype),
            pltpu.SMEM(module_kind.shape, module_kind.dtype),
            pltpu.SMEM(kind_scale.shape, kind_scale.dtype),
            pltpu.SemaphoreType.DMA((3 + pieces,)),
        ],
        cost_estimate=pl.CostEstimate(flops=0, bytes_accessed=4 * train.size, transcendentals=0),
        compiler_params=pltpu.CompilerParams(vmem_limit_bytes=32 * 2**20),
        name="stage",
    )(*(pltpu.with_memory_space_constraint(a, pltpu.HBM) for a in (train, precond, module_kind, kind_scale)))
    routes = ROUTES if sections == 4 else tuple(tuple(i ^ s for i in range(sections)) for s in range(1, sections))
    far = routes[2:]
    shape = (own_rows, cols)
    whole, half_width = jax.ShapeDtypeStruct(shape, jnp.float32), jax.ShapeDtypeStruct(shape, jnp.bfloat16)
    params = pltpu.CompilerParams(vmem_limit_bytes=48 * 2**20)
    if direct:
        part = jax.ShapeDtypeStruct((sections, *shape), jnp.float32)
        early, late = blocks[:1 + EARLY], blocks[1 + EARLY:]
        scores = pl.pallas_call(
            functools.partial(early_scores, routes),
            out_shape=part,
            in_specs=[vmem] * (len(early) + 3),
            out_specs=vmem,
            compiler_params=params,
            name="early_scores",
        )(*early, *staged)
        scores = pl.pallas_call(
            functools.partial(late_scores, routes),
            out_shape=part,
            in_specs=[vmem] * (len(late) + 4),
            out_specs=vmem,
            compiler_params=params,
            name="late_scores",
        )(*late, *staged, scores)
        own, near, swap, *aways = (scores[i] for i in range(sections))
        aways = [a.astype(jnp.bfloat16) for a in aways]
    else:
        own, near, swap, *aways = pl.pallas_call(
            functools.partial(local_scores, n, len(blocks), routes),
            out_shape=(whole, whole, whole) + (half_width,) * len(far),
            in_specs=[vmem] * (len(blocks) + 3),
            out_specs=(vmem,) * (3 + len(far)),
            scratch_shapes=[pltpu.VMEM((n * query.shape[0], feats), query.dtype)],
            compiler_params=pltpu.CompilerParams(vmem_limit_bytes=48 * 2**20),
            name="local_scores",
        )(*blocks, *staged)

    def across(x):
        return lax.ppermute(x, "half", [(0, 1), (1, 0)])

    near = (near + across(swap)).astype(jnp.bfloat16)
    for route, away in zip(far, aways):
        own = own + lax.ppermute(away, "section", list(enumerate(route))).astype(jnp.float32)
    pairs = [(2 * i + h, 2 * routes[h][i] + 1 - h) for i in range(sections) for h in range(2)]
    own = own + lax.ppermute(near, SHARDS, pairs).astype(jnp.float32)
    rows = own_rows // 2
    first = lax.axis_index("half") == 0
    mine = jnp.where(first, own[:rows], own[rows:])
    return mine + across(jnp.where(first, own[rows:], own[:rows]))


def solution(mesh):
    in_specs = (
        P("dp", SHARDS),
        P("dp", SHARDS),
        P(SHARDS, None, None),
        P(SHARDS),
        P(),
    )
    return jax.shard_map(
        per_device, mesh=mesh, in_specs=in_specs, out_specs=P(SHARDS, "dp"), check_vma=False
    )
```

```python
import functools

import jax
import jax.numpy as jnp
from jax import lax
from jax.experimental import pallas as pl
from jax.experimental.pallas import tpu as pltpu
from jax.sharding import PartitionSpec as P

SHARDS = ("section", "half")
DIRECT = 4
EARLY = 2
ROWS = 64
SHUFFLES = ((1, 3, 2, 0), (2, 1, 0, 3), (3, 0, 1, 2), (0, 2, 3, 1))
ROUTES = ((3, 2, 0, 1), (1, 0, 3, 2), (2, 3, 1, 0))


def stage(pieces, train, precond, kind, scale, train_t, precond_v, factor, raw, kind_s, scale_s, sems):
    rows = train.shape[0] // pieces
    cuts = [pl.ds(i * rows, rows) for i in range(pieces)]
    pairs = [(kind, kind_s), (scale, scale_s), (precond, precond_v)] + [(train.at[c], raw.at[c]) for c in cuts]
    copies = [pltpu.make_async_copy(src, dst, sems.at[i]) for i, (src, dst) in enumerate(pairs)]
    for c in copies:
        c.start()
    copies[0].wait()
    copies[1].wait()
    for m in range(factor.shape[0]):
        factor[m] = jnp.full(factor.shape[1:], scale_s[kind_s[m]], jnp.float32)
    for i in range(pieces):
        copies[3 + i].wait()
        train_t[:, i * rows:(i + 1) * rows] = raw[i * rows:(i + 1) * rows, :].T
    copies[2].wait()


def weighted_scores(lhs, train_t, precond, factor):
    mods, feat = precond.shape[0], precond.shape[1]
    parts = []
    for m in range(mods):
        pre = jnp.dot(lhs[:, m * feat:(m + 1) * feat], precond[m], preferred_element_type=jnp.float32)
        parts.append((pre * factor[m]).astype(jnp.bfloat16))
    return jnp.dot(jnp.concatenate(parts, axis=1), train_t[...], preferred_element_type=jnp.float32)


def destinations(routes):
    section, half = lax.axis_index("section"), lax.axis_index("half")
    to = [sum(jnp.where(section == source, target, 0) for source, target in enumerate(route)) for route in routes]
    return (section, jnp.where(half == 0, to[0], to[1]), jnp.where(half == 0, to[1], to[0]), *to[2:])


def sender(shuffle):
    dp = lax.axis_index("dp")
    return sum(jnp.where(dp == target, source, 0) for source, target in enumerate(shuffle))


def early_scores(routes, *refs):
    blocks, (train_t, precond, factor, out) = refs[:1 + EARLY], refs[1 + EARLY:]
    homes, rows = destinations(routes), blocks[0].shape[0]
    scores = weighted_scores(jnp.concatenate([b[...] for b in blocks], axis=0), train_t, precond, factor)
    owners = [lax.axis_index("dp")] + [sender(s) for s in SHUFFLES[:EARLY]]
    for i in reversed(range(1 + EARLY)):
        place = sum(jnp.where(owners[i] == home, k, 0) for k, home in enumerate(homes))
        out[place] = scores[i * rows:(i + 1) * rows]


def late_scores(routes, *refs):
    count = len(SHUFFLES) - EARLY
    blocks, (train_t, precond, factor, early, out) = refs[:count], refs[count:]
    homes, rows, dp = destinations(routes), blocks[0].shape[0], lax.axis_index("dp")
    owners = [sender(s) for s in SHUFFLES[EARLY:]]

    def add(used):
        scores = weighted_scores(jnp.concatenate([b[...] for b in blocks[:used]], axis=0), train_t, precond, factor)
        for i in range(used):
            place = sum(jnp.where(owners[i] == home, k, 0) for k, home in enumerate(homes))
            out[place] = scores[i * rows:(i + 1) * rows]

    out[...] = early[...]
    idle = owners[-1] == dp
    pl.when(idle)(lambda: add(count - 1))
    pl.when(jnp.logical_not(idle))(lambda: add(count))


def local_scores(n, blocks_in, routes, *refs):
    blocks, (train_t, precond, factor, *outs), queries = refs[:blocks_in], refs[blocks_in:-1], refs[-1]
    q_rows = queries.shape[0] // n
    own_rows = outs[0].shape[0]
    dp, section, half = (lax.axis_index(a) for a in ("dp", "section", "half"))
    to = [sum(jnp.where(section == source, target, 0) for source, target in enumerate(route)) for route in routes]
    homes = (section, jnp.where(half == 0, to[0], to[1]), jnp.where(half == 0, to[1], to[0]), *to[2:])

    if blocks_in > 1:

        def put(owner, block):
            place = sum(jnp.where(owner == home, i, 0) for i, home in enumerate(homes))
            queries[pl.ds(pl.multiple_of(place * q_rows, q_rows), q_rows), :] = block[...]

        for shuffle, block in zip(SHUFFLES, blocks[1:]):
            put(sum(jnp.where(dp == target, source, 0) for source, target in enumerate(shuffle)), block)
        put(dp, blocks[0])
        scores = weighted_scores(queries, train_t, precond, factor)
        for i, out in enumerate(outs):
            out[...] = scores[i * own_rows:(i + 1) * own_rows].astype(out.dtype)
    else:
        unit = min(q_rows, own_rows)

        def step(c, carry):
            base = pl.multiple_of(c * ROWS, ROWS)
            scores = weighted_scores(blocks[0].at[pl.ds(base, ROWS)], train_t, precond, factor)
            for i in range(ROWS // unit):
                row = base + i * unit
                at = pl.multiple_of(lax.rem(row, own_rows), unit)
                for home, out in zip(homes, outs):

                    @pl.when(row // own_rows == home)
                    def _(i=i, at=at, out=out):
                        out[pl.ds(at, unit), :] = scores[i * unit:(i + 1) * unit].astype(out.dtype)

            return carry

        lax.fori_loop(0, n * q_rows // ROWS, step, 0)


def per_device(query, train, precond, module_kind, kind_scale):
    n, sections = lax.axis_size("dp"), lax.axis_size("section")
    mods, feat = precond.shape[:2]
    cols, feats = train.shape
    own_rows = n * query.shape[0] // sections
    direct = n == sections == DIRECT
    if direct:
        blocks = [query] + [
            lax.ppermute(query, ("half", "dp"), [(n * h + i, n * (h if i != t else 1 - h) + t) for h in range(2) for i, t in enumerate(s)])
            for s in SHUFFLES
        ]
    else:
        blocks = [lax.all_gather(query, "dp", axis=0, tiled=True)]

    vmem, hbm = (pl.BlockSpec(memory_space=s) for s in (pltpu.VMEM, pltpu.HBM))
    pieces = 4
    staged = pl.pallas_call(
        functools.partial(stage, pieces),
        out_shape=(
            pltpu.VMEM((feats, cols), train.dtype),
            pltpu.VMEM(precond.shape, precond.dtype),
            pltpu.VMEM((mods, 1, feat), jnp.float32),
        ),
        in_specs=[hbm] * 4,
        out_specs=(vmem,) * 3,
        scratch_shapes=[
            pltpu.VMEM(train.shape, train.dtype),
            pltpu.SMEM(module_kind.shape, module_kind.dtype),
            pltpu.SMEM(kind_scale.shape, kind_scale.dtype),
            pltpu.SemaphoreType.DMA((3 + pieces,)),
        ],
        cost_estimate=pl.CostEstimate(flops=0, bytes_accessed=4 * train.size, transcendentals=0),
        compiler_params=pltpu.CompilerParams(vmem_limit_bytes=32 * 2**20),
        name="stage",
    )(*(pltpu.with_memory_space_constraint(a, pltpu.HBM) for a in (train, precond, module_kind, kind_scale)))
    routes = ROUTES if sections == 4 else tuple(tuple(i ^ s for i in range(sections)) for s in range(1, sections))
    far = routes[2:]
    shape = (own_rows, cols)
    whole, half_width = jax.ShapeDtypeStruct(shape, jnp.float32), jax.ShapeDtypeStruct(shape, jnp.bfloat16)
    params = pltpu.CompilerParams(vmem_limit_bytes=48 * 2**20)
    if direct:
        part = jax.ShapeDtypeStruct((sections, *shape), jnp.float32)
        early, late = blocks[:1 + EARLY], blocks[1 + EARLY:]
        scores = pl.pallas_call(
            functools.partial(early_scores, routes),
            out_shape=part,
            in_specs=[vmem] * (len(early) + 3),
            out_specs=vmem,
            compiler_params=params,
            name="early_scores",
        )(*early, *staged)
        scores = pl.pallas_call(
            functools.partial(late_scores, routes),
            out_shape=part,
            in_specs=[vmem] * (len(late) + 4),
            out_specs=vmem,
            compiler_params=params,
            name="late_scores",
        )(*late, *staged, scores)
        own, near, swap, *aways = (scores[i] for i in range(sections))
        aways = [a.astype(jnp.bfloat16) for a in aways]
    else:
        own, near, swap, *aways = pl.pallas_call(
            functools.partial(local_scores, n, len(blocks), routes),
            out_shape=(whole, whole, whole) + (half_width,) * len(far),
            in_specs=[vmem] * (len(blocks) + 3),
            out_specs=(vmem,) * (3 + len(far)),
            scratch_shapes=[pltpu.VMEM((n * query.shape[0], feats), query.dtype)],
            compiler_params=pltpu.CompilerParams(vmem_limit_bytes=48 * 2**20),
            name="local_scores",
        )(*blocks, *staged)

    def across(x):
        return lax.ppermute(x, "half", [(0, 1), (1, 0)])

    near = (near + across(swap)).astype(jnp.bfloat16)
    for route, away in zip(far, aways):
        crossed = [(2 * i + h, 2 * t + 1 - h) for i, t in enumerate(route) for h in range(2)]
        own = own + lax.ppermute(away, SHARDS, crossed).astype(jnp.float32)
    pairs = [(2 * i + h, 2 * routes[h][i] + 1 - h) for i in range(sections) for h in range(2)]
    own = own + lax.ppermute(near, SHARDS, pairs).astype(jnp.float32)
    rows = own_rows // 2
    first = lax.axis_index("half") == 0
    mine = jnp.where(first, own[:rows], own[rows:])
    return mine + across(jnp.where(first, own[rows:], own[:rows]))


def solution(mesh):
    in_specs = (
        P("dp", SHARDS),
        P("dp", SHARDS),
        P(SHARDS, None, None),
        P(SHARDS),
        P(),
    )
    return jax.shard_map(
        per_device, mesh=mesh, in_specs=in_specs, out_specs=P(SHARDS, "dp"), check_vma=False
    )
```

```python
import functools

import jax
import jax.numpy as jnp
from jax import lax
from jax.experimental import pallas as pl
from jax.experimental.pallas import tpu as pltpu
from jax.sharding import PartitionSpec as P

SHARDS = ("section", "half")
DIRECT = 4
EARLY = 2
ROWS = 64
SHUFFLES = ((1, 3, 2, 0), (2, 1, 0, 3), (3, 0, 1, 2), (0, 2, 3, 1))
ROUTES = ((3, 2, 0, 1), (1, 0, 3, 2), (2, 3, 1, 0))


def stage(pieces, train, precond, kind, scale, train_t, precond_v, factor, raw, kind_s, scale_s, sems):
    rows = train.shape[0] // pieces
    cuts = [pl.ds(i * rows, rows) for i in range(pieces)]
    pairs = [(kind, kind_s), (scale, scale_s), (precond, precond_v)] + [(train.at[c], raw.at[c]) for c in cuts]
    copies = [pltpu.make_async_copy(src, dst, sems.at[i]) for i, (src, dst) in enumerate(pairs)]
    for c in copies:
        c.start()
    copies[0].wait()
    copies[1].wait()
    for m in range(factor.shape[0]):
        factor[m] = jnp.full(factor.shape[1:], scale_s[kind_s[m]], jnp.float32)
    for i in range(pieces):
        copies[3 + i].wait()
        train_t[:, i * rows:(i + 1) * rows] = raw[i * rows:(i + 1) * rows, :].T
    copies[2].wait()


def weighted_scores(lhs, train_t, precond, factor):
    mods, feat = precond.shape[0], precond.shape[1]
    parts = []
    for m in range(mods):
        pre = jnp.dot(lhs[:, m * feat:(m + 1) * feat], precond[m], preferred_element_type=jnp.float32)
        parts.append((pre * factor[m]).astype(jnp.bfloat16))
    return jnp.dot(jnp.concatenate(parts, axis=1), train_t[...], preferred_element_type=jnp.float32)


def destinations(routes):
    section, half = lax.axis_index("section"), lax.axis_index("half")
    to = [sum(jnp.where(section == source, target, 0) for source, target in enumerate(route)) for route in routes]
    return (section, jnp.where(half == 0, to[0], to[1]), jnp.where(half == 0, to[1], to[0]), *to[2:])


def sender(shuffle):
    dp = lax.axis_index("dp")
    return sum(jnp.where(dp == target, source, 0) for source, target in enumerate(shuffle))


def early_scores(routes, *refs):
    blocks, (train_t, precond, factor, out) = refs[:1 + EARLY], refs[1 + EARLY:]
    homes, rows = destinations(routes), blocks[0].shape[0]
    scores = weighted_scores(jnp.concatenate([b[...] for b in blocks], axis=0), train_t, precond, factor)
    owners = [lax.axis_index("dp")] + [sender(s) for s in SHUFFLES[:EARLY]]
    for i in reversed(range(1 + EARLY)):
        place = sum(jnp.where(owners[i] == home, k, 0) for k, home in enumerate(homes))
        out[place] = scores[i * rows:(i + 1) * rows]


def late_scores(routes, *refs):
    count = len(SHUFFLES) - EARLY
    blocks, (train_t, precond, factor, early, out) = refs[:count], refs[count:]
    homes, rows, dp = destinations(routes), blocks[0].shape[0], lax.axis_index("dp")
    owners = [sender(s) for s in SHUFFLES[EARLY:]]

    def add(used):
        scores = weighted_scores(jnp.concatenate([b[...] for b in blocks[:used]], axis=0), train_t, precond, factor)
        for i in range(used):
            place = sum(jnp.where(owners[i] == home, k, 0) for k, home in enumerate(homes))
            out[place] = scores[i * rows:(i + 1) * rows]

    out[...] = early[...]
    idle = owners[-1] == dp
    pl.when(idle)(lambda: add(count - 1))
    pl.when(jnp.logical_not(idle))(lambda: add(count))


def local_scores(n, blocks_in, routes, *refs):
    blocks, (train_t, precond, factor, *outs), queries = refs[:blocks_in], refs[blocks_in:-1], refs[-1]
    q_rows = queries.shape[0] // n
    own_rows = outs[0].shape[0]
    dp, section, half = (lax.axis_index(a) for a in ("dp", "section", "half"))
    to = [sum(jnp.where(section == source, target, 0) for source, target in enumerate(route)) for route in routes]
    homes = (section, jnp.where(half == 0, to[0], to[1]), jnp.where(half == 0, to[1], to[0]), *to[2:])

    if blocks_in > 1:

        def put(owner, block):
            place = sum(jnp.where(owner == home, i, 0) for i, home in enumerate(homes))
            queries[pl.ds(pl.multiple_of(place * q_rows, q_rows), q_rows), :] = block[...]

        for shuffle, block in zip(SHUFFLES, blocks[1:]):
            put(sum(jnp.where(dp == target, source, 0) for source, target in enumerate(shuffle)), block)
        put(dp, blocks[0])
        scores = weighted_scores(queries, train_t, precond, factor)
        for i, out in enumerate(outs):
            out[...] = scores[i * own_rows:(i + 1) * own_rows].astype(out.dtype)
    else:
        unit = min(q_rows, own_rows)

        def step(c, carry):
            base = pl.multiple_of(c * ROWS, ROWS)
            scores = weighted_scores(blocks[0].at[pl.ds(base, ROWS)], train_t, precond, factor)
            for i in range(ROWS // unit):
                row = base + i * unit
                at = pl.multiple_of(lax.rem(row, own_rows), unit)
                for home, out in zip(homes, outs):

                    @pl.when(row // own_rows == home)
                    def _(i=i, at=at, out=out):
                        out[pl.ds(at, unit), :] = scores[i * unit:(i + 1) * unit].astype(out.dtype)

            return carry

        lax.fori_loop(0, n * q_rows // ROWS, step, 0)


def per_device(query, train, precond, module_kind, kind_scale):
    n, sections = lax.axis_size("dp"), lax.axis_size("section")
    mods, feat = precond.shape[:2]
    cols, feats = train.shape
    own_rows = n * query.shape[0] // sections
    direct = n == sections == DIRECT
    if direct:
        blocks = [query] + [
            lax.ppermute(query, ("half", "dp"), [(n * h + i, n * (h if i != t else 1 - h) + t) for h in range(2) for i, t in enumerate(s)])
            for s in SHUFFLES
        ]
    else:
        blocks = [lax.all_gather(query, "dp", axis=0, tiled=True)]

    vmem, hbm = (pl.BlockSpec(memory_space=s) for s in (pltpu.VMEM, pltpu.HBM))
    pieces = 8
    staged = pl.pallas_call(
        functools.partial(stage, pieces),
        out_shape=(
            pltpu.VMEM((feats, cols), train.dtype),
            pltpu.VMEM(precond.shape, precond.dtype),
            pltpu.VMEM((mods, 1, feat), jnp.float32),
        ),
        in_specs=[hbm] * 4,
        out_specs=(vmem,) * 3,
        scratch_shapes=[
            pltpu.VMEM(train.shape, train.dtype),
            pltpu.SMEM(module_kind.shape, module_kind.dtype),
            pltpu.SMEM(kind_scale.shape, kind_scale.dtype),
            pltpu.SemaphoreType.DMA((3 + pieces,)),
        ],
        cost_estimate=pl.CostEstimate(flops=0, bytes_accessed=4 * train.size, transcendentals=0),
        compiler_params=pltpu.CompilerParams(vmem_limit_bytes=32 * 2**20),
        name="stage",
    )(*(pltpu.with_memory_space_constraint(a, pltpu.HBM) for a in (train, precond, module_kind, kind_scale)))
    routes = ROUTES if sections == 4 else tuple(tuple(i ^ s for i in range(sections)) for s in range(1, sections))
    far = routes[2:]
    shape = (own_rows, cols)
    whole, half_width = jax.ShapeDtypeStruct(shape, jnp.float32), jax.ShapeDtypeStruct(shape, jnp.bfloat16)
    params = pltpu.CompilerParams(vmem_limit_bytes=48 * 2**20)
    if direct:
        part = jax.ShapeDtypeStruct((sections, *shape), jnp.float32)
        early, late = blocks[:1 + EARLY], blocks[1 + EARLY:]
        scores = pl.pallas_call(
            functools.partial(early_scores, routes),
            out_shape=part,
            in_specs=[vmem] * (len(early) + 3),
            out_specs=vmem,
            compiler_params=params,
            name="early_scores",
        )(*early, *staged)
        scores = pl.pallas_call(
            functools.partial(late_scores, routes),
            out_shape=part,
            in_specs=[vmem] * (len(late) + 4),
            out_specs=vmem,
            compiler_params=params,
            name="late_scores",
        )(*late, *staged, scores)
        own, near, swap, *aways = (scores[i] for i in range(sections))
        aways = [a.astype(jnp.bfloat16) for a in aways]
    else:
        own, near, swap, *aways = pl.pallas_call(
            functools.partial(local_scores, n, len(blocks), routes),
            out_shape=(whole, whole, whole) + (half_width,) * len(far),
            in_specs=[vmem] * (len(blocks) + 3),
            out_specs=(vmem,) * (3 + len(far)),
            scratch_shapes=[pltpu.VMEM((n * query.shape[0], feats), query.dtype)],
            compiler_params=pltpu.CompilerParams(vmem_limit_bytes=48 * 2**20),
            name="local_scores",
        )(*blocks, *staged)

    def across(x):
        return lax.ppermute(x, "half", [(0, 1), (1, 0)])

    near = (near + across(swap)).astype(jnp.bfloat16)
    for route, away in zip(far, aways):
        own = own + lax.ppermute(away, "section", list(enumerate(route))).astype(jnp.float32)
    pairs = [(2 * i + h, 2 * routes[h][i] + 1 - h) for i in range(sections) for h in range(2)]
    own = own + lax.ppermute(near, SHARDS, pairs).astype(jnp.float32)
    rows = own_rows // 2
    first = lax.axis_index("half") == 0
    mine = jnp.where(first, own[:rows], own[rows:])
    return mine + across(jnp.where(first, own[rows:], own[:rows]))


def solution(mesh):
    in_specs = (
        P("dp", SHARDS),
        P("dp", SHARDS),
        P(SHARDS, None, None),
        P(SHARDS),
        P(),
    )
    return jax.shard_map(
        per_device, mesh=mesh, in_specs=in_specs, out_specs=P(SHARDS, "dp"), check_vma=False
    )
```
